32 devices in a mesh: sx: 2 (over x), sy: 4 (over y, core), ta: 4 (over z).
Axes of the slice: x: 2, y: 2, z: 4, core: 2. Of those that a mesh axis runs over, the one named last changes fastest.
Arguments:
- velocity: bfloat16 [3, 256, 8, 1024], P(None, 'ta', 'sx', 'sy'), may hold values from -6 to 6
- seeds_first: int32 [64, 64], replicated, may hold values from -64 to 64
- seeds_merge: int32 [2, 128, 64], replicated, may hold values from -64 to 64
Outputs:
- basis: float32 [64, 5, 8, 1024], P(None, None, 'sx', ('sy', 'ta'))
The draws below stay inside these ranges and needn't reach their ends.
All inputs are finite; a program needn't handle non-finite values.
Results may differ from the reference program's by a relative error of at most 0.0008.
Values may be sent and summed in bfloat16 or wider, within the bound.
A program may use at most 64 MiB of HBM per device.

```python
import jax
import jax.numpy as jnp
from jax import lax

RANK = 64
LEVELS = 2
NX = 8
NY = 1024
SNAPS = 256
N_TA = 4


def touch_ends(entries, own_key, low, largest):
    extent = entries.shape
    place = [jax.random.randint(jax.random.fold_in(own_key, axis), (), 0, extent[axis]) for axis in range(len(extent))]
    entries = entries.at[tuple(place)].set(low)
    longest = extent.index(max(extent))
    place[longest] = (place[longest] + 1) % extent[longest]
    return entries.at[tuple(place)].set(largest)


def levels(key, shape, split, smallest, largest):
    loudness, own = 1.0, jax.random.fold_in(key, 6)
    for dim, blocks in split:
        draws = jnp.exp(jax.random.uniform(jax.random.fold_in(own, dim), (blocks,), jnp.float32, smallest / len(split), largest / len(split)))
        loudness = loudness * jnp.repeat(draws, shape[dim] // blocks).reshape([-1 if axis == dim else 1 for axis in range(len(shape))])
    return loudness


def noise(stream_key, dims, spread, bound, split=(), kind=jnp.bfloat16):
    gain = levels(stream_key, dims, split, -0.22, 0.18) if split else 1.0
    result = jax.random.normal(stream_key, dims, jnp.float32) * spread * gain
    return jnp.minimum(jnp.maximum(result, -bound), bound).astype(kind)


def setup_inputs(seed: int = 0) -> dict:
    streams_of = jax.random.split(jax.random.key(seed), 4)
    return {
        "velocity": noise(streams_of[0], (3, SNAPS, NX, NY), 1.0, 6.0, ((1, 4), (2, 2), (3, 4))),
        "seeds_first": touch_ends(jax.random.randint(streams_of[1], (RANK, RANK), -64, 65), jax.random.fold_in(streams_of[1], 1), -64, 64).astype(jnp.int32),
        "seeds_merge": touch_ends(jax.random.randint(streams_of[2], (LEVELS, 2 * RANK, RANK), -64, 65), jax.random.fold_in(streams_of[2], 1), -64, 64).astype(jnp.int32),
    }


def matmul_hi(left, right):
    return jnp.dot(left, right, precision=lax.Precision.HIGHEST)

def coefficients(gram_mat, rotation):
    order_n = gram_mat.shape[0]
    scaling = jnp.sqrt(jnp.trace(gram_mat) / order_n)
    imaged = matmul_hi(gram_mat, rotation)
    reduced = matmul_hi(rotation.T, imaged)
    factor = jnp.linalg.cholesky(reduced)
    solved = jax.scipy.linalg.solve_triangular(factor, imaged.T, lower=True)
    return solved.T / scaling

def diff_x(field):
    return 0.5 * (field[:, 2:, 1:-1] - field[:, :-2, 1:-1])

def diff_y(field):
    return 0.5 * (field[:, 1:-1, 2:] - field[:, 1:-1, :-2])

def strain_rows(padded):
    comp_u = padded[0]
    comp_v = padded[1]
    comp_w = padded[2]
    fields = jnp.stack([diff_x(comp_u), diff_y(comp_v), 0.5 * (diff_y(comp_u) + diff_x(comp_v)), 0.5 * diff_x(comp_w), 0.5 * diff_y(comp_w)], axis=1)
    return fields.reshape(fields.shape[0], -1)

def rotations(seeds_first, seeds_merge):
    width = seeds_first.shape[0]
    first = jnp.eye(width, dtype=jnp.float32) + seeds_first.astype(jnp.float32) * (0.5 / (64.0 * 8.0))
    stacked = jnp.concatenate([jnp.eye(width, dtype=jnp.float32), jnp.eye(width, dtype=jnp.float32)], axis=0) / jnp.sqrt(jnp.float32(2.0))
    merges = stacked[None] + seeds_merge.astype(jnp.float32) * (0.5 / (64.0 * jnp.sqrt(jnp.float32(128.0))))
    return (first, merges)

def reference(velocity, seeds_first, seeds_merge):
    rotation_first, rotation_merge = rotations(seeds_first, seeds_merge)
    bases = []
    for blk_idx in range(N_TA):
        snap_block = velocity[:, blk_idx * RANK:(blk_idx + 1) * RANK].astype(jnp.float32)
        padded = jnp.pad(snap_block, ((0, 0), (0, 0), (1, 1), (1, 1)))
        strain = strain_rows(padded)
        gram_mat = matmul_hi(strain, strain.T)
        kmat = coefficients(gram_mat, rotation_first)
        bases.append(matmul_hi(kmat.T, strain))
    for depth_at in range(LEVELS):
        merged = []
        for pair_idx in range(len(bases) // 2):
            stacked = jnp.concatenate([bases[2 * pair_idx], bases[2 * pair_idx + 1]], axis=0)
            gram_mat = matmul_hi(stacked, stacked.T)
            kmat = coefficients(gram_mat, rotation_merge[depth_at])
            merged.append(matmul_hi(kmat.T, stacked))
        bases = merged
    return bases[0].reshape(RANK, 5, NX, NY)
```

```python
import jax
import jax.numpy as jnp
from jax import lax
from jax.experimental import pallas as pl
from jax.experimental.pallas import tpu as pltpu
from jax.sharding import PartitionSpec as P

HI = lax.Precision.HIGHEST


def mm(left, right, contract=(1, 0)):
    return lax.dot_general(
        left,
        right,
        (((contract[0],), (contract[1],)), ((), ())),
        precision=HI,
        preferred_element_type=jnp.float32,
    )


def eye(rows, cols):
    return (
        lax.broadcasted_iota(jnp.int32, (rows, cols), 0)
        == lax.broadcasted_iota(jnp.int32, (rows, cols), 1)
    ).astype(jnp.float32)


def inverse_factors(mats):
    n = mats[0].shape[0]
    batch = len(mats)
    tiles = n // 8
    ident = eye(n, n)
    width = 2 * n
    work = [
        [jnp.concatenate([m, ident], axis=1)[8 * i : 8 * i + 8] for i in range(tiles)]
        for m in mats
    ]
    sub = lax.broadcasted_iota(jnp.int32, (8, width), 0)
    done = [[None] * tiles for _ in range(batch)]
    for p in range(tiles):
        cols = [
            [
                [
                    jnp.broadcast_to(work[b][i][:, 8 * p + k : 8 * p + k + 1], (8, width))
                    for i in range(p, tiles)
                ]
                for k in range(8)
            ]
            for b in range(batch)
        ]
        for b in range(batch):
            head = work[b][p]
            rest = [work[b][i] for i in range(p + 1, tiles)]
            scales = jnp.zeros((8, width), jnp.float32)
            for k in range(8):
                pivot = cols[b][k][0][k : k + 1]
                inv = 1.0 / pivot
                scales = jnp.where(sub == k, jnp.broadcast_to(inv, (8, width)), scales)
                row = head[k : k + 1] * inv
                across = [cols[b][j][0][k : k + 1] * inv for j in range(k + 1, 8)]
                below = jnp.where(sub > k, cols[b][k][0], 0.0)
                head = head - below * row
                for j in range(k + 1, 8):
                    cols[b][j][0] = cols[b][j][0] - below * across[j - k - 1]
                for i in range(1, tiles - p):
                    factor = cols[b][k][i]
                    rest[i - 1] = rest[i - 1] - factor * row
                    for j in range(k + 1, 8):
                        cols[b][j][i] = cols[b][j][i] - factor * across[j - k - 1]
            done[b][p] = head * jnp.sqrt(scales)
            for i in range(p + 1, tiles):
                work[b][i] = rest[i - p - 1]
    return [jnp.concatenate(done[b], axis=0)[:, n:] for b in range(batch)]


def solve_steps(grams, rotation):
    order_n = rotation.shape[0]
    ident = eye(order_n, order_n)
    imaged = [mm(g, rotation) for g in grams]
    reduced = [mm(rotation, z, (0, 0)) for z in imaged]
    inverses = inverse_factors(reduced)
    out = []
    for g, z, inverse in zip(grams, imaged, inverses):
        trace = jnp.sum(jnp.sum(g * ident, axis=0, keepdims=True), axis=1, keepdims=True)
        out.append(mm(inverse, z, (1, 1)) * lax.rsqrt(trace / order_n))
    return out


def block_diagonal(low, high):
    zero_low = jnp.zeros((low.shape[0], high.shape[1]), jnp.float32)
    zero_high = jnp.zeros((high.shape[0], low.shape[1]), jnp.float32)
    return jnp.concatenate(
        [
            jnp.concatenate([low, zero_low], axis=1),
            jnp.concatenate([zero_high, high], axis=1),
        ],
        axis=0,
    )


def tree_kernel(gram_ref, strain_ref, first_ref, merge_ref, out_ref):
    width = first_ref.shape[0]
    num_levels = merge_ref.shape[0]
    blocks = gram_ref.shape[0] // width
    first = eye(width, width) + first_ref[...].astype(jnp.float32) * (0.5 / 512.0)
    span = width
    coefs = solve_steps(
        [gram_ref[b * span : (b + 1) * span, b * span : (b + 1) * span] for b in range(blocks)],
        first,
    )
    stacked = jnp.concatenate([eye(width, width)] * 2, axis=0) * (2.0**-0.5)
    for level in range(num_levels):
        rotation = stacked + merge_ref[level].astype(jnp.float32) * (0.5 / (64.0 * 128.0**0.5))
        span *= 2
        pairs = [block_diagonal(coefs[2 * i], coefs[2 * i + 1]) for i in range(len(coefs) // 2)]
        grams = []
        for i, pair in enumerate(pairs):
            part = gram_ref[i * span : (i + 1) * span, i * span : (i + 1) * span]
            grams.append(mm(mm(pair, part), pair, (1, 1)))
        solved = solve_steps(grams, rotation)
        coefs = [mm(kt, pair) for kt, pair in zip(solved, pairs)]
    out_ref[...] = mm(coefs[0], strain_ref[...])


def padded_2(x, sides, width):
    for axis, dim in sides:
        size, length = (lax.axis_size(axis), x.shape[dim])
        up = [(i, (i + 1) % size) for i in range(size - 1)]
        down = [(j, i) for i, j in up]
        last = lax.slice_in_dim(x, length - width, length, axis=dim)
        leading = lax.slice_in_dim(x, 0, width, axis=dim)
        before = lax.ppermute(last, axis, up)
        after = lax.ppermute(leading, axis, down)
        x = jnp.concatenate([before, x, after], axis=dim)
    return x


def diff_x(field):
    return 0.5 * (field[:, 2:, 1:-1] - field[:, :-2, 1:-1])


def diff_y(field):
    return 0.5 * (field[:, 1:-1, 2:] - field[:, 1:-1, :-2])


def strain_rows(padded):
    comp_u = padded[0]
    comp_v = padded[1]
    comp_w = padded[2]
    fields = jnp.stack(
        [
            diff_x(comp_u),
            diff_y(comp_v),
            0.5 * (diff_y(comp_u) + diff_x(comp_v)),
            0.5 * diff_x(comp_w),
            0.5 * diff_y(comp_w),
        ],
        axis=1,
    )
    return fields.reshape(fields.shape[0], -1)


def local(velocity, seeds_first, seeds_merge):
    width = seeds_first.shape[0]
    cells_x = velocity.shape[2]
    cells_y = velocity.shape[3]
    blocks = lax.axis_size("ta")
    quarter = cells_y // blocks
    rimmed = padded_2(velocity, (("sx", 2), ("sy", 3)), 1)
    pieces = jnp.stack(
        [rimmed[..., i * quarter : (i + 1) * quarter + 2] for i in range(blocks)], axis=0
    )
    pieces = lax.all_to_all(pieces, "ta", 0, 0, tiled=True)
    pieces = pieces.transpose(1, 0, 2, 3, 4).reshape(
        3, blocks * width, cells_x + 2, quarter + 2
    )
    strain = strain_rows(pieces.astype(jnp.float32))
    gram = lax.psum(jnp.dot(strain, strain.T, precision=HI), ("sx", "sy", "ta"))
    vmem = pl.BlockSpec(memory_space=pltpu.VMEM)
    out = pl.pallas_call(
        tree_kernel,
        out_shape=jax.ShapeDtypeStruct((width, strain.shape[1]), jnp.float32),
        in_specs=[vmem] * 4,
        out_specs=vmem,
        compiler_params=pltpu.CompilerParams(vmem_limit_bytes=32 * 2**20),
        name="tree",
    )(gram, strain, seeds_first, seeds_merge)
    return out.reshape(width, 5, cells_x, quarter)


def solution(mesh):
    in_specs = (P(None, "ta", "sx", "sy"), P(), P())
    out_specs = P(None, None, "sx", ("sy", "ta"))
    return jax.shard_map(local, mesh=mesh, in_specs=in_specs, out_specs=out_specs, check_vma=False)
```

```python
import functools

import jax
import jax.numpy as jnp
from jax import lax
from jax.experimental import pallas as pl
from jax.experimental.pallas import tpu as pltpu
from jax.sharding import PartitionSpec as P

HI = lax.Precision.HIGHEST


def mm(left, right, contract=(1, 0)):
    return lax.dot_general(
        left,
        right,
        (((contract[0],), (contract[1],)), ((), ())),
        precision=HI,
        preferred_element_type=jnp.float32,
    )


def eye(rows, cols):
    return (
        lax.broadcasted_iota(jnp.int32, (rows, cols), 0)
        == lax.broadcasted_iota(jnp.int32, (rows, cols), 1)
    ).astype(jnp.float32)


def inverse_factors(mats):
    n = mats[0].shape[0]
    batch = len(mats)
    tiles = n // 8
    ident = eye(n, n)
    width = 2 * n
    work = [
        [jnp.concatenate([m, ident], axis=1)[8 * i : 8 * i + 8] for i in range(tiles)]
        for m in mats
    ]
    sub = lax.broadcasted_iota(jnp.int32, (8, width), 0)
    done = [[None] * tiles for _ in range(batch)]
    for p in range(tiles):
        cols = [
            [
                [
                    jnp.broadcast_to(work[b][i][:, 8 * p + k : 8 * p + k + 1], (8, width))
                    for i in range(p, tiles)
                ]
                for k in range(8)
            ]
            for b in range(batch)
        ]
        for b in range(batch):
            head = work[b][p]
            rest = [work[b][i] for i in range(p + 1, tiles)]
            scales = jnp.zeros((8, width), jnp.float32)
            for k in range(8):
                pivot = cols[b][k][0][k : k + 1]
                inv = 1.0 / pivot
                scales = jnp.where(sub == k, jnp.broadcast_to(inv, (8, width)), scales)
                row = head[k : k + 1] * inv
                across = [cols[b][j][0][k : k + 1] * inv for j in range(k + 1, 8)]
                below = jnp.where(sub > k, cols[b][k][0], 0.0)
                head = head - below * row
                for j in range(k + 1, 8):
                    cols[b][j][0] = cols[b][j][0] - below * across[j - k - 1]
                for i in range(1, tiles - p):
                    factor = cols[b][k][i]
                    rest[i - 1] = rest[i - 1] - factor * row
                    for j in range(k + 1, 8):
                        cols[b][j][i] = cols[b][j][i] - factor * across[j - k - 1]
            done[b][p] = head * jnp.sqrt(scales)
            for i in range(p + 1, tiles):
                work[b][i] = rest[i - p - 1]
    return [jnp.concatenate(done[b], axis=0)[:, n:] for b in range(batch)]


def solve_steps(grams, rotation):
    order_n = rotation.shape[0]
    ident = eye(order_n, order_n)
    imaged = [mm(g, rotation) for g in grams]
    reduced = [mm(rotation, z, (0, 0)) for z in imaged]
    inverses = inverse_factors(reduced)
    out = []
    for g, z, inverse in zip(grams, imaged, inverses):
        trace = jnp.sum(jnp.sum(g * ident, axis=0, keepdims=True), axis=1, keepdims=True)
        out.append(mm(inverse, z, (1, 1)) * lax.rsqrt(trace / order_n))
    return out


def block_diagonal(low, high):
    zero_low = jnp.zeros((low.shape[0], high.shape[1]), jnp.float32)
    zero_high = jnp.zeros((high.shape[0], low.shape[1]), jnp.float32)
    return jnp.concatenate(
        [
            jnp.concatenate([low, zero_low], axis=1),
            jnp.concatenate([zero_high, high], axis=1),
        ],
        axis=0,
    )


def tree_kernel(gram_ref, strain_ref, first_ref, merge_ref, out_ref):
    width = first_ref.shape[0]
    pair = 2 * width
    gram_low = gram_ref[:pair]
    gram_cross = gram_ref[pair : 2 * pair]
    gram_high = gram_ref[2 * pair : 3 * pair]
    first = eye(width, width) + first_ref[...].astype(jnp.float32) * (0.5 / 512.0)
    stacked = jnp.concatenate([eye(width, width)] * 2, axis=0) * (2.0**-0.5)
    turns = [
        stacked + merge_ref[level].astype(jnp.float32) * (0.5 / (64.0 * 128.0**0.5))
        for level in range(2)
    ]
    coefs = solve_steps(
        [g[i * width : (i + 1) * width, i * width : (i + 1) * width] for g in (gram_low, gram_high) for i in (0, 1)],
        first,
    )
    low, high = block_diagonal(coefs[0], coefs[1]), block_diagonal(coefs[2], coefs[3])
    solved = solve_steps(
        [mm(mm(low, gram_low), low, (1, 1)), mm(mm(high, gram_high), high, (1, 1))], turns[0]
    )
    low, high = mm(solved[0], low), mm(solved[1], high)
    cross = mm(mm(high, gram_cross), low, (1, 1))
    top = jnp.concatenate([mm(mm(low, gram_low), low, (1, 1)), cross.T], axis=1)
    bottom = jnp.concatenate([cross, mm(mm(high, gram_high), high, (1, 1))], axis=1)
    last = solve_steps([jnp.concatenate([top, bottom], axis=0)], turns[1])[0]
    weights = jnp.concatenate([mm(last[:, :width], low), mm(last[:, width:], high)], axis=1)
    out_ref[...] = mm(weights, strain_ref[...])


MESH = pl.DeviceIdType.MESH


def loop(start, stop, body):
    if stop - start <= 8:
        for i in range(start, stop):
            body(i)
    else:
        lax.fori_loop(start, stop, lambda i, carry: (body(i), carry)[1], 0)


def dot16(left, right, contract=(1, 0)):
    return lax.dot_general(
        left,
        right,
        (((contract[0],), (contract[1],)), ((), ())),
        preferred_element_type=jnp.float32,
    )


def iotas(rows, cols):
    return (
        lax.broadcasted_iota(jnp.int32, (rows, cols), 0),
        lax.broadcasted_iota(jnp.int32, (rows, cols), 1),
    )


def signed_half(plus, minus):
    return (0.5 * plus.astype(jnp.float32) - 0.5 * minus.astype(jnp.float32)).astype(jnp.bfloat16)


def gather_kernel(
    quarter, nx, ny, nt,
    chunk_ref, strain_ref, gram_ref,
    held, from_up, from_down, edges, from_left, from_right, parts, landed, slices, whole,
    chunk_sems, x_sems, y_sems, rim_sems, scatter_sems, line_sems, spread_sems,
):
    ix, iy, it = lax.axis_index("sx"), lax.axis_index("sy"), lax.axis_index("ta")
    plane = nx * ny
    me = ix * ny + iy
    rows3, lanes = chunk_ref.shape[1:]
    snaps = rows3 // 3
    cells_x = lanes // quarter

    def plane_peer(j):
        t = lax.rem(me + j, plane)
        return t, (t // ny, lax.rem(t, ny), it)

    def ta_peer(d):
        t = lax.rem(it + d, nt)
        return t, (ix, iy, t)

    def copy(src, dst, sems, index, device):
        return pltpu.make_async_remote_copy(
            src_ref=src, dst_ref=dst, send_sem=sems.at[0, index], recv_sem=sems.at[1, index],
            device_id=device, device_id_type=MESH,
        )

    barrier = pltpu.get_barrier_semaphore()

    def greet(device):
        pl.semaphore_signal(barrier, inc=1, device_id=device, device_id_type=MESH)

    loop(1, plane, lambda j: greet(plane_peer(j)[1]))
    for d in range(1, nt):
        greet(ta_peer(d)[1])
    right_ok, left_ok = iy + 1 < ny, iy > 0
    first, last = it == 0, it == nt - 1

    @pl.when(jnp.logical_and(right_ok, it > 0))
    def _():
        greet((ix, iy + 1, 0))

    @pl.when(jnp.logical_and(left_ok, it < nt - 1))
    def _():
        greet((ix, iy - 1, nt - 1))

    @pl.when(jnp.logical_and(left_ok, first))
    def _():
        for b in range(1, nt):
            greet((ix, iy - 1, b))

    @pl.when(jnp.logical_and(right_ok, last))
    def _():
        for b in range(nt - 1):
            greet((ix, iy + 1, b))

    extra = (
        jnp.where(right_ok, jnp.where(last, nt - 1, 0) + jnp.where(it > 0, 1, 0), 0)
        + jnp.where(left_ok, jnp.where(first, nt - 1, 0) + jnp.where(it < nt - 1, 1, 0), 0)
    )
    pl.semaphore_wait(barrier, plane - 1 + nt - 1 + extra)

    def chunk_copy(d, arriving=False):
        t, device = ta_peer(d)
        slot = lax.rem(it - d + nt, nt) if arriving else it
        return copy(chunk_ref.at[t], held.at[slot], chunk_sems, d, device)

    for d in range(1, nt):
        chunk_copy(d).start()
    held[it] = chunk_ref[it]

    row, lane = iotas(16, lanes)
    column = jnp.where(
        row < cells_x, row * quarter, (row - cells_x) * quarter + quarter - 1
    )
    column = jnp.where(row < 2 * cells_x, column, -1)
    select = (lane == column).astype(jnp.float32).astype(jnp.bfloat16)
    for q in range(nt):
        edges[q] = dot16(select, chunk_ref[q], (1, 1)).astype(jnp.bfloat16)

    def left_copy(d):
        q, device = ta_peer(d)
        return q > 0, copy(edges.at[jnp.maximum(q - 1, 0)], from_left.at[it], y_sems, d, device)

    def right_copy(d):
        q, device = ta_peer(d)
        return q < nt - 1, copy(
            edges.at[jnp.minimum(q + 1, nt - 1)], from_right.at[it], y_sems, nt + d, device
        )

    def rim_copies():
        up = (ix, jnp.minimum(iy + 1, ny - 1), 0)
        down = (ix, jnp.maximum(iy - 1, 0), nt - 1)
        return (
            (right_ok, copy(edges.at[nt - 1], from_left.at[it], rim_sems, it, up)),
            (left_ok, copy(edges.at[0], from_right.at[it], rim_sems, nt + it, down)),
        )

    def each_edge(act):
        for d in range(1, nt):
            for cond, c in (left_copy(d), right_copy(d)):
                pl.when(cond)(functools.partial(act, c))
        for cond, c in rim_copies():
            pl.when(cond)(functools.partial(act, c))

    each_edge(lambda c: c.start())

    @pl.when(it > 0)
    def _():
        from_left[it] = edges[jnp.maximum(it - 1, 0)]

    @pl.when(it < nt - 1)
    def _():
        from_right[it] = edges[jnp.minimum(it + 1, nt - 1)]

    @pl.when(jnp.logical_and(first, jnp.logical_not(left_ok)))
    def _():
        from_left[...] = jnp.zeros_like(from_left)

    @pl.when(jnp.logical_and(last, jnp.logical_not(right_ok)))
    def _():
        from_right[...] = jnp.zeros_like(from_right)

    def x_copies(d):
        b = lax.rem(it - d + nt, nt)
        up = (jnp.minimum(ix + 1, nx - 1), iy, it)
        down = (jnp.maximum(ix - 1, 0), iy, it)
        return (
            (ix < nx - 1, copy(held.at[b, :, pl.ds(lanes - 128, 128)], from_up.at[b], x_sems, d, up)),
            (ix > 0, copy(held.at[b, :, pl.ds(0, 128)], from_down.at[b], x_sems, nt + d, down)),
        )

    @pl.when(ix == 0)
    def _():
        from_up[...] = jnp.zeros_like(from_up)

    @pl.when(ix == nx - 1)
    def _():
        from_down[...] = jnp.zeros_like(from_down)

    for d in range(nt):
        if d:
            chunk_copy(d, True).wait_recv()
        for cond, c in x_copies(d):
            pl.when(cond)(functools.partial(lambda c: c.start(), c))

    row, lane = iotas(lanes, lanes)
    gap = row - lane
    same = row // quarter == lane // quarter
    both = jnp.concatenate(
        [
            signed_half(gap == quarter, gap == -quarter),
            signed_half((gap == 1) & same, (gap == -1) & same),
        ],
        axis=1,
    )
    row, lane = iotas(128, lanes)
    none = row < 0
    above = signed_half(none, (row - (128 - quarter) == lane) & (row >= 128 - quarter))
    below = signed_half((lane - (lanes - quarter) == row) & (row < quarter), none)
    row, lane = iotas(16, lanes)
    none = row < 0
    left = signed_half(
        none, (row >= cells_x) & (row < 2 * cells_x) & (lane == (row - cells_x) * quarter)
    )
    right = signed_half((row < cells_x) & (lane == row * quarter + quarter - 1), none)

    @pl.when(it > 0)
    def _():
        for d in range(1, nt):
            b = lax.rem(it - d + nt, nt)
            copy(edges.at[0], from_left.at[b], y_sems, d, (ix, iy, b)).wait_recv()

    @pl.when(it < nt - 1)
    def _():
        for d in range(1, nt):
            b = lax.rem(it - d + nt, nt)
            copy(edges.at[0], from_right.at[b], y_sems, nt + d, (ix, iy, b)).wait_recv()

    @pl.when(jnp.logical_and(first, left_ok))
    def _():
        for b in range(nt):
            copy(edges.at[0], from_left.at[b], rim_sems, b, (ix, iy - 1, b)).wait_recv()

    @pl.when(jnp.logical_and(last, right_ok))
    def _():
        for b in range(nt):
            copy(edges.at[0], from_right.at[b], rim_sems, nt + b, (ix, iy + 1, b)).wait_recv()

    @pl.when(ix > 0)
    def _():
        for d in range(nt):
            b = lax.rem(it - d + nt, nt)
            copy(
                held.at[b, :, pl.ds(lanes - 128, 128)], from_up.at[b], x_sems, d, (ix - 1, iy, it)
            ).wait_recv()

    @pl.when(ix < nx - 1)
    def _():
        for d in range(nt):
            b = lax.rem(it - d + nt, nt)
            copy(
                held.at[b, :, pl.ds(0, 128)], from_down.at[b], x_sems, nt + d, (ix + 1, iy, it)
            ).wait_recv()

    for b in range(nt):
        inner = dot16(held[b], both)
        dx = inner[:, :lanes] + dot16(from_up[b], above) + dot16(from_down[b], below)
        dy = inner[:, lanes:] + dot16(from_left[b], left, (0, 0)) + dot16(from_right[b], right, (0, 0))
        ux, vx, wx = (dx[i * snaps : (i + 1) * snaps] for i in range(3))
        uy, vy, wy = (dy[i * snaps : (i + 1) * snaps] for i in range(3))
        for k, field in enumerate((ux, vy, 0.5 * (uy + vx), 0.5 * wx, 0.5 * wy)):
            strain_ref[b * snaps : (b + 1) * snaps, k * lanes : (k + 1) * lanes] = field

    strain = strain_ref[...]
    coarse = strain.astype(jnp.bfloat16)
    fine = (strain - coarse.astype(jnp.float32)).astype(jnp.bfloat16)
    half = nt * snaps // 2
    blocks = []
    for a, b in ((0, 0), (1, 0), (1, 1)):
        ra, rb = slice(a * half, (a + 1) * half), slice(b * half, (b + 1) * half)
        blocks.append(
            dot16(coarse[ra], coarse[rb], (1, 1))
            + (dot16(coarse[ra], fine[rb], (1, 1)) + dot16(fine[ra], coarse[rb], (1, 1)))
        )
    share = parts.shape[1]
    spare = plane * share - 3 * half
    if spare:
        blocks.append(jnp.zeros((spare, 128), jnp.float32))
    parts[...] = jnp.concatenate(blocks, axis=0).reshape(plane, share, 128)

    def scatter_copy(j):
        t, device = plane_peer(j)
        return copy(parts.at[t], landed.at[j], scatter_sems, j, device)

    loop(1, plane, lambda j: scatter_copy(j).start())
    landed[0] = parts[me]
    loop(1, plane, lambda j: scatter_copy(j).wait_recv())
    slices[it] = jnp.sum(landed[...], axis=0)

    for d in range(1, nt):
        copy(slices.at[it], slices.at[it], line_sems, d, ta_peer(d)[1]).start()
    for d in range(1, nt):
        b = lax.rem(it - d + nt, nt)
        copy(slices.at[it], slices.at[b], line_sems, d, ta_peer(d)[1]).wait_recv()
    whole[me] = jnp.sum(slices[...], axis=0)

    loop(1, plane, lambda j: copy(whole.at[me], whole.at[me], spread_sems, j, plane_peer(j)[1]).start())

    def arrive(j):
        t = lax.rem(me - j + plane, plane)
        copy(whole.at[me], whole.at[t], spread_sems, j, plane_peer(j)[1]).wait_recv()

    loop(1, plane, arrive)
    gram_ref[...] = whole[...].reshape(plane * share, 128)

    for d in range(1, nt):
        chunk_copy(d).wait_send()
        copy(slices.at[it], slices.at[it], line_sems, d, ta_peer(d)[1]).wait_send()
    each_edge(lambda c: c.wait_send())
    for d in range(nt):
        for cond, c in x_copies(d):
            pl.when(cond)(functools.partial(lambda c: c.wait_send(), c))
    loop(1, plane, lambda j: scatter_copy(j).wait_send())
    loop(1, plane, lambda j: copy(whole.at[me], whole.at[me], spread_sems, j, plane_peer(j)[1]).wait_send())


def local(velocity, seeds_first, seeds_merge):
    comps, width, cells_x, cells_y = velocity.shape
    nx, ny, nt = (lax.axis_size(a) for a in ("sx", "sy", "ta"))
    quarter = cells_y // nt
    lanes = cells_x * quarter
    plane = nx * ny
    share = -(-3 * 2 * width // (8 * plane)) * 8
    chunks = velocity.reshape(comps, width, cells_x, nt, quarter).transpose(3, 0, 1, 2, 4)
    chunks = chunks.reshape(nt, comps * width, lanes)
    rows3 = comps * width
    vmem = pl.BlockSpec(memory_space=pltpu.VMEM)
    b16, f32 = jnp.bfloat16, jnp.float32
    dma = pltpu.SemaphoreType.DMA
    strain, gram = pl.pallas_call(
        functools.partial(gather_kernel, quarter, nx, ny, nt),
        out_shape=(
            jax.ShapeDtypeStruct((nt * width, 5 * lanes), f32),
            jax.ShapeDtypeStruct((plane * share, 128), f32),
        ),
        in_specs=[vmem],
        out_specs=(vmem, vmem),
        scratch_shapes=[
            pltpu.VMEM((nt, rows3, lanes), b16),
            pltpu.VMEM((nt, rows3, 128), b16),
            pltpu.VMEM((nt, rows3, 128), b16),
            pltpu.VMEM((nt, 16, rows3), b16),
            pltpu.VMEM((nt, 16, rows3), b16),
            pltpu.VMEM((nt, 16, rows3), b16),
            pltpu.VMEM((plane, share, 128), f32),
            pltpu.VMEM((plane, share, 128), f32),
            pltpu.VMEM((nt, share, 128), f32),
            pltpu.VMEM((plane, share, 128), f32),
            dma((2, nt)),
            dma((2, 2 * nt)),
            dma((2, 2 * nt)),
            dma((2, 2 * nt)),
            dma((2, plane)),
            dma((2, nt)),
            dma((2, plane)),
        ],
        compiler_params=pltpu.CompilerParams(
            collective_id=0, has_side_effects=True, vmem_limit_bytes=32 * 2**20
        ),
        name="gather",
    )(chunks)
    out = pl.pallas_call(
        tree_kernel,
        out_shape=jax.ShapeDtypeStruct((width, 5 * lanes), f32),
        in_specs=[vmem] * 4,
        out_specs=vmem,
        compiler_params=pltpu.CompilerParams(vmem_limit_bytes=32 * 2**20),
        name="tree",
    )(gram, strain, seeds_first, seeds_merge)
    return out.reshape(width, 5, cells_x, quarter)


def solution(mesh):
    in_specs = (P(None, "ta", "sx", "sy"), P(), P())
    out_specs = P(None, None, "sx", ("sy", "ta"))
    return jax.shard_map(local, mesh=mesh, in_specs=in_specs, out_specs=out_specs, check_vma=False)
```

```python
import functools

import jax
import jax.numpy as jnp
from jax import lax
from jax.experimental import pallas as pl
from jax.experimental.pallas import tpu as pltpu
from jax.sharding import PartitionSpec as P

HI = lax.Precision.HIGHEST


def mm(left, right, contract=(1, 0)):
    return lax.dot_general(
        left,
        right,
        (((contract[0],), (contract[1],)), ((), ())),
        precision=HI,
        preferred_element_type=jnp.float32,
    )


def eye(rows, cols):
    return (
        lax.broadcasted_iota(jnp.int32, (rows, cols), 0)
        == lax.broadcasted_iota(jnp.int32, (rows, cols), 1)
    ).astype(jnp.float32)


def inverse_factors(mats):
    n = mats[0].shape[0]
    batch = len(mats)
    tiles = n // 8
    ident = eye(n, n)
    width = 2 * n
    work = [
        [jnp.concatenate([m, ident], axis=1)[8 * i : 8 * i + 8] for i in range(tiles)]
        for m in mats
    ]
    sub = lax.broadcasted_iota(jnp.int32, (8, width), 0)
    done = [[None] * tiles for _ in range(batch)]
    for p in range(tiles):
        cols = [
            [
                [
                    jnp.broadcast_to(work[b][i][:, 8 * p + k : 8 * p + k + 1], (8, width))
                    for i in range(p, tiles)
                ]
                for k in range(8)
            ]
            for b in range(batch)
        ]
        for b in range(batch):
            head = work[b][p]
            rest = [work[b][i] for i in range(p + 1, tiles)]
            scales = jnp.zeros((8, width), jnp.float32)
            for k in range(8):
                pivot = cols[b][k][0][k : k + 1]
                inv = 1.0 / pivot
                scales = jnp.where(sub == k, jnp.broadcast_to(inv, (8, width)), scales)
                row = head[k : k + 1] * inv
                across = [cols[b][j][0][k : k + 1] * inv for j in range(k + 1, 8)]
                below = jnp.where(sub > k, cols[b][k][0], 0.0)
                head = head - below * row
                for j in range(k + 1, 8):
                    cols[b][j][0] = cols[b][j][0] - below * across[j - k - 1]
                for i in range(1, tiles - p):
                    factor = cols[b][k][i]
                    rest[i - 1] = rest[i - 1] - factor * row
                    for j in range(k + 1, 8):
                        cols[b][j][i] = cols[b][j][i] - factor * across[j - k - 1]
            done[b][p] = head * jnp.sqrt(scales)
            for i in range(p + 1, tiles):
                work[b][i] = rest[i - p - 1]
    return [jnp.concatenate(done[b], axis=0)[:, n:] for b in range(batch)]


def solve_steps(grams, rotation):
    order_n = rotation.shape[0]
    ident = eye(order_n, order_n)
    imaged = [mm(g, rotation) for g in grams]
    reduced = [mm(rotation, z, (0, 0)) for z in imaged]
    inverses = inverse_factors(reduced)
    out = []
    for g, z, inverse in zip(grams, imaged, inverses):
        trace = jnp.sum(jnp.sum(g * ident, axis=0, keepdims=True), axis=1, keepdims=True)
        out.append(mm(inverse, z, (1, 1)) * lax.rsqrt(trace / order_n))
    return out


def block_diagonal(low, high):
    zero_low = jnp.zeros((low.shape[0], high.shape[1]), jnp.float32)
    zero_high = jnp.zeros((high.shape[0], low.shape[1]), jnp.float32)
    return jnp.concatenate(
        [
            jnp.concatenate([low, zero_low], axis=1),
            jnp.concatenate([zero_high, high], axis=1),
        ],
        axis=0,
    )


def tree_kernel(gram_ref, strain_ref, first_ref, merge_ref, out_ref):
    width = first_ref.shape[0]
    pair = 2 * width
    gram_low = gram_ref[:pair]
    gram_cross = gram_ref[pair : 2 * pair]
    gram_high = gram_ref[2 * pair : 3 * pair]
    first = eye(width, width) + first_ref[...].astype(jnp.float32) * (0.5 / 512.0)
    stacked = jnp.concatenate([eye(width, width)] * 2, axis=0) * (2.0**-0.5)
    turns = [
        stacked + merge_ref[level].astype(jnp.float32) * (0.5 / (64.0 * 128.0**0.5))
        for level in range(2)
    ]
    coefs = solve_steps(
        [g[i * width : (i + 1) * width, i * width : (i + 1) * width] for g in (gram_low, gram_high) for i in (0, 1)],
        first,
    )
    low, high = block_diagonal(coefs[0], coefs[1]), block_diagonal(coefs[2], coefs[3])
    solved = solve_steps(
        [mm(mm(low, gram_low), low, (1, 1)), mm(mm(high, gram_high), high, (1, 1))], turns[0]
    )
    low, high = mm(solved[0], low), mm(solved[1], high)
    cross = mm(mm(high, gram_cross), low, (1, 1))
    top = jnp.concatenate([mm(mm(low, gram_low), low, (1, 1)), cross.T], axis=1)
    bottom = jnp.concatenate([cross, mm(mm(high, gram_high), high, (1, 1))], axis=1)
    last = solve_steps([jnp.concatenate([top, bottom], axis=0)], turns[1])[0]
    weights = jnp.concatenate([mm(last[:, :width], low), mm(last[:, width:], high)], axis=1)
    out_ref[...] = mm(weights, strain_ref[...])


MESH = pl.DeviceIdType.MESH


def loop(start, stop, body):
    if stop - start <= 8:
        for i in range(start, stop):
            body(i)
    else:
        lax.fori_loop(start, stop, lambda i, carry: (body(i), carry)[1], 0)


def dot16(left, right, contract=(1, 0)):
    return lax.dot_general(
        left,
        right,
        (((contract[0],), (contract[1],)), ((), ())),
        preferred_element_type=jnp.float32,
    )


def iotas(rows, cols):
    return (
        lax.broadcasted_iota(jnp.int32, (rows, cols), 0),
        lax.broadcasted_iota(jnp.int32, (rows, cols), 1),
    )


def signed_half(plus, minus):
    return (0.5 * plus.astype(jnp.float32) - 0.5 * minus.astype(jnp.float32)).astype(jnp.bfloat16)


def gather_kernel(
    quarter, nx, ny, nt,
    velocity_ref, strain_ref, gram_ref,
    chunk_ref, held, from_up, from_down, edges, from_left, from_right, parts, landed, slices, whole,
    chunk_sems, x_sems, y_sems, rim_sems, scatter_sems, line_sems, spread_sems,
):
    ix, iy, it = lax.axis_index("sx"), lax.axis_index("sy"), lax.axis_index("ta")
    plane = nx * ny
    me = ix * ny + iy
    rows3, lanes = chunk_ref.shape[1:]
    snaps = rows3 // 3
    cells_x = lanes // quarter

    def plane_peer(j):
        t = lax.rem(me + j, plane)
        return t, (t // ny, lax.rem(t, ny), it)

    def ta_peer(d):
        t = lax.rem(it + d, nt)
        return t, (ix, iy, t)

    def copy(src, dst, sems, index, device):
        return pltpu.make_async_remote_copy(
            src_ref=src, dst_ref=dst, send_sem=sems.at[0, index], recv_sem=sems.at[1, index],
            device_id=device, device_id_type=MESH,
        )

    barrier = pltpu.get_barrier_semaphore()

    def greet(device):
        pl.semaphore_signal(barrier, inc=1, device_id=device, device_id_type=MESH)

    loop(1, plane, lambda j: greet(plane_peer(j)[1]))
    for d in range(1, nt):
        greet(ta_peer(d)[1])
    right_ok, left_ok = iy + 1 < ny, iy > 0
    first, last = it == 0, it == nt - 1

    @pl.when(jnp.logical_and(right_ok, it > 0))
    def _():
        greet((ix, iy + 1, 0))

    @pl.when(jnp.logical_and(left_ok, it < nt - 1))
    def _():
        greet((ix, iy - 1, nt - 1))

    @pl.when(jnp.logical_and(left_ok, first))
    def _():
        for b in range(1, nt):
            greet((ix, iy - 1, b))

    @pl.when(jnp.logical_and(right_ok, last))
    def _():
        for b in range(nt - 1):
            greet((ix, iy + 1, b))

    extra = (
        jnp.where(right_ok, jnp.where(last, nt - 1, 0) + jnp.where(it > 0, 1, 0), 0)
        + jnp.where(left_ok, jnp.where(first, nt - 1, 0) + jnp.where(it < nt - 1, 1, 0), 0)
    )

    for c in range(3):
        field = velocity_ref[c].astype(jnp.float32)
        rows = [field[:, x, :] for x in range(cells_x)]
        for q in range(nt):
            piece = jnp.concatenate([r[:, q * quarter : (q + 1) * quarter] for r in rows], axis=1)
            chunk_ref[q, c * snaps : (c + 1) * snaps] = piece.astype(jnp.bfloat16)
    pl.semaphore_wait(barrier, plane - 1 + nt - 1 + extra)

    def chunk_copy(d, arriving=False):
        t, device = ta_peer(d)
        slot = lax.rem(it - d + nt, nt) if arriving else it
        return copy(chunk_ref.at[t], held.at[slot], chunk_sems, d, device)

    for d in range(1, nt):
        chunk_copy(d).start()
    held[it] = chunk_ref[it]

    row, lane = iotas(16, lanes)
    column = jnp.where(
        row < cells_x, row * quarter, (row - cells_x) * quarter + quarter - 1
    )
    column = jnp.where(row < 2 * cells_x, column, -1)
    select = (lane == column).astype(jnp.float32).astype(jnp.bfloat16)
    for q in range(nt):
        edges[q] = dot16(select, chunk_ref[q], (1, 1)).astype(jnp.bfloat16)

    def left_copy(d):
        q, device = ta_peer(d)
        return q > 0, copy(edges.at[jnp.maximum(q - 1, 0)], from_left.at[it], y_sems, d, device)

    def right_copy(d):
        q, device = ta_peer(d)
        return q < nt - 1, copy(
            edges.at[jnp.minimum(q + 1, nt - 1)], from_right.at[it], y_sems, nt + d, device
        )

    def rim_copies():
        up = (ix, jnp.minimum(iy + 1, ny - 1), 0)
        down = (ix, jnp.maximum(iy - 1, 0), nt - 1)
        return (
            (right_ok, copy(edges.at[nt - 1], from_left.at[it], rim_sems, it, up)),
            (left_ok, copy(edges.at[0], from_right.at[it], rim_sems, nt + it, down)),
        )

    def each_edge(act):
        for d in range(1, nt):
            for cond, c in (left_copy(d), right_copy(d)):
                pl.when(cond)(functools.partial(act, c))
        for cond, c in rim_copies():
            pl.when(cond)(functools.partial(act, c))

    each_edge(lambda c: c.start())

    @pl.when(it > 0)
    def _():
        from_left[it] = edges[jnp.maximum(it - 1, 0)]

    @pl.when(it < nt - 1)
    def _():
        from_right[it] = edges[jnp.minimum(it + 1, nt - 1)]

    @pl.when(jnp.logical_and(first, jnp.logical_not(left_ok)))
    def _():
        from_left[...] = jnp.zeros_like(from_left)

    @pl.when(jnp.logical_and(last, jnp.logical_not(right_ok)))
    def _():
        from_right[...] = jnp.zeros_like(from_right)

    def x_copies(d):
        b = lax.rem(it - d + nt, nt)
        up = (jnp.minimum(ix + 1, nx - 1), iy, it)
        down = (jnp.maximum(ix - 1, 0), iy, it)
        return (
            (ix < nx - 1, copy(held.at[b, :, pl.ds(lanes - 128, 128)], from_up.at[b], x_sems, d, up)),
            (ix > 0, copy(held.at[b, :, pl.ds(0, 128)], from_down.at[b], x_sems, nt + d, down)),
        )

    @pl.when(ix == 0)
    def _():
        from_up[...] = jnp.zeros_like(from_up)

    @pl.when(ix == nx - 1)
    def _():
        from_down[...] = jnp.zeros_like(from_down)

    for d in range(nt):
        if d:
            chunk_copy(d, True).wait_recv()
        for cond, c in x_copies(d):
            pl.when(cond)(functools.partial(lambda c: c.start(), c))

    row, lane = iotas(lanes, lanes)
    gap = row - lane
    same = row // quarter == lane // quarter
    both = jnp.concatenate(
        [
            signed_half(gap == quarter, gap == -quarter),
            signed_half((gap == 1) & same, (gap == -1) & same),
        ],
        axis=1,
    )
    row, lane = iotas(128, lanes)
    none = row < 0
    above = signed_half(none, (row - (128 - quarter) == lane) & (row >= 128 - quarter))
    below = signed_half((lane - (lanes - quarter) == row) & (row < quarter), none)
    row, lane = iotas(16, lanes)
    none = row < 0
    left = signed_half(
        none, (row >= cells_x) & (row < 2 * cells_x) & (lane == (row - cells_x) * quarter)
    )
    right = signed_half((row < cells_x) & (lane == row * quarter + quarter - 1), none)

    @pl.when(it > 0)
    def _():
        for d in range(1, nt):
            b = lax.rem(it - d + nt, nt)
            copy(edges.at[0], from_left.at[b], y_sems, d, (ix, iy, b)).wait_recv()

    @pl.when(it < nt - 1)
    def _():
        for d in range(1, nt):
            b = lax.rem(it - d + nt, nt)
            copy(edges.at[0], from_right.at[b], y_sems, nt + d, (ix, iy, b)).wait_recv()

    @pl.when(jnp.logical_and(first, left_ok))
    def _():
        for b in range(nt):
            copy(edges.at[0], from_left.at[b], rim_sems, b, (ix, iy - 1, b)).wait_recv()

    @pl.when(jnp.logical_and(last, right_ok))
    def _():
        for b in range(nt):
            copy(edges.at[0], from_right.at[b], rim_sems, nt + b, (ix, iy + 1, b)).wait_recv()

    @pl.when(ix > 0)
    def _():
        for d in range(nt):
            b = lax.rem(it - d + nt, nt)
            copy(
                held.at[b, :, pl.ds(lanes - 128, 128)], from_up.at[b], x_sems, d, (ix - 1, iy, it)
            ).wait_recv()

    @pl.when(ix < nx - 1)
    def _():
        for d in range(nt):
            b = lax.rem(it - d + nt, nt)
            copy(
                held.at[b, :, pl.ds(0, 128)], from_down.at[b], x_sems, nt + d, (ix + 1, iy, it)
            ).wait_recv()

    for b in range(nt):
        inner = dot16(held[b], both)
        dx = inner[:, :lanes] + dot16(from_up[b], above) + dot16(from_down[b], below)
        dy = inner[:, lanes:] + dot16(from_left[b], left, (0, 0)) + dot16(from_right[b], right, (0, 0))
        ux, vx, wx = (dx[i * snaps : (i + 1) * snaps] for i in range(3))
        uy, vy, wy = (dy[i * snaps : (i + 1) * snaps] for i in range(3))
        for k, field in enumerate((ux, vy, 0.5 * (uy + vx), 0.5 * wx, 0.5 * wy)):
            strain_ref[b * snaps : (b + 1) * snaps, k * lanes : (k + 1) * lanes] = field

    strain = strain_ref[...]
    coarse = strain.astype(jnp.bfloat16)
    fine = (strain - coarse.astype(jnp.float32)).astype(jnp.bfloat16)
    half = nt * snaps // 2
    blocks = []
    for a, b in ((0, 0), (1, 0), (1, 1)):
        ra, rb = slice(a * half, (a + 1) * half), slice(b * half, (b + 1) * half)
        blocks.append(
            dot16(coarse[ra], coarse[rb], (1, 1))
            + (dot16(coarse[ra], fine[rb], (1, 1)) + dot16(fine[ra], coarse[rb], (1, 1)))
        )
    share = parts.shape[1]
    spare = plane * share - 3 * half
    if spare:
        blocks.append(jnp.zeros((spare, 128), jnp.float32))
    parts[...] = jnp.concatenate(blocks, axis=0).reshape(plane, share, 128)

    def scatter_copy(j):
        t, device = plane_peer(j)
        return copy(parts.at[t], landed.at[j], scatter_sems, j, device)

    loop(1, plane, lambda j: scatter_copy(j).start())
    landed[0] = parts[me]
    loop(1, plane, lambda j: scatter_copy(j).wait_recv())
    slices[it] = jnp.sum(landed[...], axis=0)

    for d in range(1, nt):
        copy(slices.at[it], slices.at[it], line_sems, d, ta_peer(d)[1]).start()
    for d in range(1, nt):
        b = lax.rem(it - d + nt, nt)
        copy(slices.at[it], slices.at[b], line_sems, d, ta_peer(d)[1]).wait_recv()
    whole[me] = jnp.sum(slices[...], axis=0)

    loop(1, plane, lambda j: copy(whole.at[me], whole.at[me], spread_sems, j, plane_peer(j)[1]).start())

    def arrive(j):
        t = lax.rem(me - j + plane, plane)
        copy(whole.at[me], whole.at[t], spread_sems, j, plane_peer(j)[1]).wait_recv()

    loop(1, plane, arrive)
    gram_ref[...] = whole[...].reshape(plane * share, 128)

    for d in range(1, nt):
        chunk_copy(d).wait_send()
        copy(slices.at[it], slices.at[it], line_sems, d, ta_peer(d)[1]).wait_send()
    each_edge(lambda c: c.wait_send())
    for d in range(nt):
        for cond, c in x_copies(d):
            pl.when(cond)(functools.partial(lambda c: c.wait_send(), c))
    loop(1, plane, lambda j: scatter_copy(j).wait_send())
    loop(1, plane, lambda j: copy(whole.at[me], whole.at[me], spread_sems, j, plane_peer(j)[1]).wait_send())


def local(velocity, seeds_first, seeds_merge):
    comps, width, cells_x, cells_y = velocity.shape
    nx, ny, nt = (lax.axis_size(a) for a in ("sx", "sy", "ta"))
    quarter = cells_y // nt
    lanes = cells_x * quarter
    plane = nx * ny
    share = -(-3 * 2 * width // (8 * plane)) * 8
    rows3 = comps * width
    vmem = pl.BlockSpec(memory_space=pltpu.VMEM)
    b16, f32 = jnp.bfloat16, jnp.float32
    dma = pltpu.SemaphoreType.DMA
    strain, gram = pl.pallas_call(
        functools.partial(gather_kernel, quarter, nx, ny, nt),
        out_shape=(
            jax.ShapeDtypeStruct((nt * width, 5 * lanes), f32),
            jax.ShapeDtypeStruct((plane * share, 128), f32),
        ),
        in_specs=[vmem],
        out_specs=(vmem, vmem),
        scratch_shapes=[
            pltpu.VMEM((nt, rows3, lanes), b16),
            pltpu.VMEM((nt, rows3, lanes), b16),
            pltpu.VMEM((nt, rows3, 128), b16),
            pltpu.VMEM((nt, rows3, 128), b16),
            pltpu.VMEM((nt, 16, rows3), b16),
            pltpu.VMEM((nt, 16, rows3), b16),
            pltpu.VMEM((nt, 16, rows3), b16),
            pltpu.VMEM((plane, share, 128), f32),
            pltpu.VMEM((plane, share, 128), f32),
            pltpu.VMEM((nt, share, 128), f32),
            pltpu.VMEM((plane, share, 128), f32),
            dma((2, nt)),
            dma((2, 2 * nt)),
            dma((2, 2 * nt)),
            dma((2, 2 * nt)),
            dma((2, plane)),
            dma((2, nt)),
            dma((2, plane)),
        ],
        compiler_params=pltpu.CompilerParams(
            collective_id=0, has_side_effects=True, vmem_limit_bytes=32 * 2**20
        ),
        name="gather",
    )(velocity)
    out = pl.pallas_call(
        tree_kernel,
        out_shape=jax.ShapeDtypeStruct((width, 5 * lanes), f32),
        in_specs=[vmem] * 4,
        out_specs=vmem,
        compiler_params=pltpu.CompilerParams(vmem_limit_bytes=32 * 2**20),
        name="tree",
    )(gram, strain, seeds_first, seeds_merge)
    return out.reshape(width, 5, cells_x, quarter)


def solution(mesh):
    in_specs = (P(None, "ta", "sx", "sy"), P(), P())
    out_specs = P(None, None, "sx", ("sy", "ta"))
    return jax.shard_map(local, mesh=mesh, in_specs=in_specs, out_specs=out_specs, check_vma=False)
```
